32 devices in a mesh: panel: 8 (over z, core), tm: 4 (over y, x).
Axes of the slice: x: 2, y: 2, z: 4, core: 2. Of those that a mesh axis runs over, the one named last changes fastest.
Arguments:
- pressures: bfloat16 [49152, 3072], P('panel', 'tm'), may hold values from -60 to 60
- sketch: bfloat16 [49152, 128], P(('panel', 'tm')), may hold values from -6 to 6
Outputs:
- basis_rows: bfloat16 [3072, 128], P('tm')
- image: float32 [49152, 128], P(('panel', 'tm'))
The draws below stay inside these ranges and needn't reach their ends.
All inputs are finite; a program needn't handle non-finite values.
Results may differ from the reference program's by a relative error of at most 0.0029.
Values may be sent and summed in bfloat16 or wider, within the bound.
A program may use at most 64 MiB of HBM per device.

```python
import jax
import jax.numpy as jnp
from jax import lax

K = 128
NP = 49152
NT = 3072


def draw_pressures(key, part):
    keys = jax.random.split(key, 3)
    row_scale = jnp.exp(jax.random.uniform(keys[0], (NP, 1), jnp.float32, jnp.log(0.3), jnp.log(3.0)))
    col_scale = jnp.exp(jax.random.uniform(keys[1], (1, NT), jnp.float32, jnp.log(0.3), jnp.log(3.0)))
    base = jnp.clip(jax.random.normal(keys[2], (NP, NT), jnp.float32), -6.0, 6.0)
    return (base * row_scale * col_scale).astype(jnp.bfloat16)


def shard_levels(key, dims, pieces, least, largest):
    factor_of = 1.0
    for position, shards_of in pieces:
        steps = jax.random.uniform(jax.random.fold_in(jax.random.fold_in(key, 6), position), (shards_of,), jnp.float32, least / len(pieces), largest / len(pieces))
        factor_of = factor_of * jnp.repeat(jnp.exp(steps), dims[position] // shards_of).reshape((-1,) + (1,) * (len(dims) - 1 - position))
    return factor_of


def centred(rng, extent, deviation, bound, shards=(), held_as=jnp.bfloat16):
    drawn = deviation * jax.random.normal(rng, extent, jnp.float32)
    if shards:
        drawn = drawn * shard_levels(rng, extent, shards, -0.22, 0.18)
    return jnp.clip(drawn, -bound, bound).astype(held_as)


def setup_inputs(seed: int = 0) -> dict:
    seeds = jax.random.split(jax.random.key(seed), 3)
    return {
        "pressures": draw_pressures(jax.random.fold_in(seeds[2], 71), 0),
        "sketch": centred(seeds[1], (NP, K), 1.0, 6.0, ((0, 32),)),
    }


def reference(pressures, sketch):
    y_full = lax.dot_general(pressures.astype(jnp.float32), sketch.astype(jnp.float32), (((0,), (0,)), ((), ())), preferred_element_type=jnp.float32)
    gram_matrix = lax.dot_general(y_full.astype(jnp.float32), y_full.astype(jnp.float32), (((0,), (0,)), ((), ())), precision=lax.Precision.HIGHEST, preferred_element_type=jnp.float32)
    lower_factor = jnp.linalg.cholesky(gram_matrix)
    solved = jax.scipy.linalg.solve_triangular(lower_factor, y_full.T, lower=True)
    basis_rows = solved.T.astype(jnp.bfloat16)
    image = jnp.dot(pressures.astype(jnp.float32), basis_rows.astype(jnp.float32), preferred_element_type=jnp.float32)
    return (basis_rows, image)
```

```python
import functools

import jax
import jax.numpy as jnp
from jax import lax
from jax.experimental import pallas as pl
from jax.experimental.pallas import tpu as pltpu
from jax.sharding import PartitionSpec as P

MESH = pl.DeviceIdType.MESH
F32 = jnp.float32
BF16 = jnp.bfloat16
HIGHEST = lax.Precision.HIGHEST


def flipped(index, offset):
    bit = 1
    while bit <= offset:
        if offset & bit:
            index = index + bit - 2 * bit * lax.rem(lax.div(index, bit), 2)
        bit *= 2
    return index


def inverse_factor(aug, linv):
    k = linv.shape[0]
    sub = lax.broadcasted_iota(jnp.int32, (8, 2 * k), 0)
    for base in range(0, k, 8):
        block = aug[base : base + 8, :]
        s = {}
        for j in range(8):
            column = jnp.broadcast_to(block[:, base + j : base + j + 1], (8, k))
            for i in range(j, 8):
                s[i, j] = jnp.broadcast_to(column[i : i + 1, :], (8, k))
        rows = [jnp.broadcast_to(block[i : i + 1, :], (8, 2 * k)) for i in range(8)]
        recip = []
        for j in range(8):
            recip.append(1.0 / s[j, j])
            for i in range(j + 1, 8):
                m = s[i, j] * recip[j]
                for l in range(j + 1, i + 1):
                    s[i, l] = s[i, l] - m * s[l, j]
                rows[i] = rows[i] - jnp.concatenate([m, m], axis=1) * rows[j]
        done = rows[0]
        scale = recip[0]
        root = lax.rsqrt(s[0, 0])
        for j in range(1, 8):
            done = jnp.where(sub == j, rows[j], done)
            scale = jnp.where(sub[:, :k] == j, recip[j], scale)
            root = jnp.where(sub[:, :k] == j, lax.rsqrt(s[j, j]), root)
        linv[base : base + 8, :] = done[:, k:] * root
        if base + 8 < k:
            scaled = (done[:, :k] * scale).T[base + 8 :, :]
            aug[base + 8 :, :] = aug[base + 8 :, :] - jnp.dot(
                scaled, done, precision=HIGHEST, preferred_element_type=F32
            )


def kernel(
    n_panel, n_tm, p_hbm, s_hbm, basis_ref, image_ref,
    p_all, s_all, yt, y_full, core_in, z_in, g_own, g_in, aug, linv, basis, out_part, in_part, image,
    load_sem, s_load, s_send, s_recv, c_send, c_recv, z_send, z_recv, a_send, a_recv,
    b_send, b_recv, g_send, g_recv, o_send, o_recv, store_sem,
):
    panel, tm = lax.axis_index("panel"), lax.axis_index("tm")
    z, core = lax.div(panel, 2), lax.rem(panel, 2)
    n_z = n_panel // 2
    own = s_hbm.shape[0]
    k = s_hbm.shape[1]
    piece = k // n_panel
    half = k // 2

    def tm_partner(o):
        return (panel, flipped(tm, o))

    def z_partner(o):
        return (2 * flipped(z, o) + core, tm)

    other = (2 * z + 1 - core, tm)
    partners = [tm_partner(o) for o in range(1, n_tm)] + [z_partner(o) for o in range(1, n_z)] + [other]

    loads = []
    for o in range(n_tm):
        start = pl.multiple_of(flipped(tm, o) * own, own)
        load = pltpu.make_async_copy(p_hbm.at[pl.ds(start, own), :], p_all.at[o], load_sem.at[o])
        load.start()
        loads.append(load)
    own_load = pltpu.make_async_copy(s_hbm, s_all.at[0], s_load)
    own_load.start()

    barrier = pltpu.get_barrier_semaphore()
    for where in partners:
        pl.semaphore_signal(barrier, inc=1, device_id=where, device_id_type=MESH)
    pl.semaphore_wait(barrier, len(partners))

    def remote(src, dst, send, recv, where):
        copy = pltpu.make_async_remote_copy(
            src_ref=src, dst_ref=dst, send_sem=send, recv_sem=recv, device_id=where, device_id_type=MESH
        )
        copy.start()
        return copy

    sent = [
        remote(s_hbm, s_all.at[o], s_send.at[o], s_recv.at[o], tm_partner(o)) for o in range(1, n_tm)
    ]

    for o in range(n_tm):
        if o == 0:
            own_load.wait()
        else:
            sent[o - 1].wait_recv()
        loads[o].wait()
        product = lax.dot_general(
            s_all[o], p_all[o], (((0,), (0,)), ((), ())), preferred_element_type=F32
        )
        if o == 0:
            yt[...] = product
        else:
            yt[...] += product

    mine = pl.multiple_of(core * half, half)
    theirs = pl.multiple_of((1 - core) * half, half)
    copy = remote(yt.at[pl.ds(theirs, half), :], core_in, c_send, c_recv, other)
    copy.wait()
    yt[pl.ds(mine, half), :] += core_in[...]
    at = pl.multiple_of(mine + z * piece, piece)
    copies = []
    for o in range(1, n_z):
        there = pl.multiple_of(mine + flipped(z, o) * piece, piece)
        copies.append(remote(yt.at[pl.ds(there, piece), :], z_in.at[o], z_send.at[o], z_recv.at[o], z_partner(o)))
    total = yt[pl.ds(at, piece), :]
    for o in range(1, n_z):
        copies[o - 1].wait()
        total = total + z_in[o]
    y_full[pl.ds(at, piece), :] = total
    gathered = y_full.at[pl.ds(at, piece), :]
    copies = [
        remote(gathered, gathered, a_send.at[o], a_recv.at[o], z_partner(o)) for o in range(1, n_z)
    ]
    for copy in copies:
        copy.wait()
    gathered = y_full.at[pl.ds(mine, half), :]
    remote(gathered, gathered, b_send, b_recv, other).wait()

    rows = y_full[...]
    g_own[...] = lax.dot_general(
        rows, rows, (((1,), (1,)), ((), ())), precision=HIGHEST, preferred_element_type=F32
    )
    copies = [
        remote(g_own, g_in.at[o], g_send.at[o], g_recv.at[o], tm_partner(o)) for o in range(1, n_tm)
    ]
    gram = g_own[...]
    for o in range(1, n_tm):
        copies[o - 1].wait()
        gram = gram + g_in[o]
    aug[:, :k] = gram
    aug[:, k:] = (
        lax.broadcasted_iota(jnp.int32, (k, k), 0) == lax.broadcasted_iota(jnp.int32, (k, k), 1)
    ).astype(F32)
    inverse_factor(aug, linv)
    basis_t = jnp.dot(linv[...], y_full[...], precision=HIGHEST, preferred_element_type=F32)
    basis[...] = basis_t.T.astype(BF16)
    basis_store = pltpu.make_async_copy(basis, basis_ref, store_sem.at[0])
    basis_store.start()

    copies = []
    for o in range(n_tm - 1, 0, -1):
        out_part[o] = jnp.dot(p_all[o], basis[...], preferred_element_type=F32).astype(BF16)
        copies.append(remote(out_part.at[o], in_part.at[o], o_send.at[o], o_recv.at[o], tm_partner(o)))
    image[...] = jnp.dot(p_all[0], basis[...], preferred_element_type=F32)
    for o, copy in zip(range(n_tm - 1, 0, -1), copies):
        copy.wait()
        image[...] += in_part[o].astype(F32)
    store = pltpu.make_async_copy(image, image_ref, store_sem.at[1])
    store.start()
    for copy in sent:
        copy.wait_send()
    basis_store.wait()
    store.wait()


def on_device(n_panel, n_tm, pressures, sketch):
    own, k = sketch.shape
    nt = pressures.shape[1]
    n_z = n_panel // 2
    dma = pltpu.SemaphoreType.DMA
    return pl.pallas_call(
        functools.partial(kernel, n_panel, n_tm),
        out_shape=(jax.ShapeDtypeStruct((nt, k), BF16), jax.ShapeDtypeStruct((own, k), F32)),
        in_specs=[pl.BlockSpec(memory_space=pl.ANY)] * 2,
        out_specs=(pl.BlockSpec(memory_space=pl.ANY),) * 2,
        scratch_shapes=[
            pltpu.VMEM((n_tm, own, nt), BF16),
            pltpu.VMEM((n_tm, own, k), BF16),
            pltpu.VMEM((k, nt), F32),
            pltpu.VMEM((k, nt), F32),
            pltpu.VMEM((k // 2, nt), F32),
            pltpu.VMEM((n_z, k // n_panel, nt), F32),
            pltpu.VMEM((k, k), F32),
            pltpu.VMEM((n_tm, k, k), F32),
            pltpu.VMEM((k, 2 * k), F32),
            pltpu.VMEM((k, k), F32),
            pltpu.VMEM((nt, k), BF16),
            pltpu.VMEM((n_tm, own, k), BF16),
            pltpu.VMEM((n_tm, own, k), BF16),
            pltpu.VMEM((own, k), F32),
            dma((n_tm,)), dma, dma((n_tm,)), dma((n_tm,)),
            dma, dma, dma((n_z,)), dma((n_z,)), dma((n_z,)), dma((n_z,)),
            dma, dma, dma((n_tm,)), dma((n_tm,)), dma((n_tm,)), dma((n_tm,)), dma((2,)),
        ],
        compiler_params=pltpu.CompilerParams(
            collective_id=0, has_side_effects=True, vmem_limit_bytes=48 * 1024 * 1024
        ),
        cost_estimate=pl.CostEstimate(
            flops=4 * pressures.shape[0] * nt * k, bytes_accessed=2 * pressures.size, transcendentals=0
        ),
    )(pressures, sketch)


def solution(mesh):
    return jax.shard_map(
        functools.partial(on_device, mesh.shape["panel"], mesh.shape["tm"]),
        mesh=mesh,
        in_specs=(P("panel", "tm"), P(("panel", "tm"), None)),
        out_specs=(P("tm", None), P(("panel", "tm"), None)),
        check_vma=False,
    )
```

```python
import functools

import jax
import jax.numpy as jnp
from jax import lax
from jax.experimental import pallas as pl
from jax.experimental.pallas import tpu as pltpu
from jax.sharding import PartitionSpec as P

MESH = pl.DeviceIdType.MESH
F32 = jnp.float32
BF16 = jnp.bfloat16
HIGHEST = lax.Precision.HIGHEST


def flipped(index, offset):
    bit = 1
    while bit <= offset:
        if offset & bit:
            index = index + bit - 2 * bit * lax.rem(lax.div(index, bit), 2)
        bit *= 2
    return index


def inverse_factor(aug, linv):
    k = linv.shape[0]
    sub = lax.broadcasted_iota(jnp.int32, (8, 2 * k), 0)
    for base in range(0, k, 8):
        block = aug[base : base + 8, :]
        s = {}
        for j in range(8):
            column = jnp.broadcast_to(block[:, base + j : base + j + 1], (8, k))
            for i in range(j, 8):
                s[i, j] = jnp.broadcast_to(column[i : i + 1, :], (8, k))
        rows = [jnp.broadcast_to(block[i : i + 1, :], (8, 2 * k)) for i in range(8)]
        recip = []
        for j in range(8):
            recip.append(1.0 / s[j, j])
            for i in range(j + 1, 8):
                m = s[i, j] * recip[j]
                for l in range(j + 1, i + 1):
                    s[i, l] = s[i, l] - m * s[l, j]
                rows[i] = rows[i] - jnp.concatenate([m, m], axis=1) * rows[j]
        done = rows[0]
        scale = recip[0]
        root = lax.rsqrt(s[0, 0])
        for j in range(1, 8):
            done = jnp.where(sub == j, rows[j], done)
            scale = jnp.where(sub[:, :k] == j, recip[j], scale)
            root = jnp.where(sub[:, :k] == j, lax.rsqrt(s[j, j]), root)
        linv[base : base + 8, :] = done[:, k:] * root
        if base + 8 < k:
            scaled = (done[:, :k] * scale).T[base + 8 :, :]
            aug[base + 8 :, :] = aug[base + 8 :, :] - jnp.dot(
                scaled, done, precision=HIGHEST, preferred_element_type=F32
            )


def kernel(
    n_panel, n_tm, p_hbm, s_hbm, basis_ref, image_ref,
    p_all, s_all, yt, y_full, core_in, z_in, g_own, g_in, aug, linv, basis, out_part, in_part, image,
    load_sem, s_load, s_send, s_recv, c_send, c_recv, z_send, z_recv, a_send, a_recv,
    b_send, b_recv, g_send, g_recv, o_send, o_recv, store_sem,
):
    panel, tm = lax.axis_index("panel"), lax.axis_index("tm")
    z, core = lax.div(panel, 2), lax.rem(panel, 2)
    n_z = n_panel // 2
    own = s_hbm.shape[0]
    k = s_hbm.shape[1]
    piece = k // n_panel
    half = k // 2

    def tm_partner(o):
        return (panel, flipped(tm, o))

    def z_partner(o):
        return (2 * flipped(z, o) + core, tm)

    other = (2 * z + 1 - core, tm)
    partners = [tm_partner(o) for o in range(1, n_tm)] + [z_partner(o) for o in range(1, n_z)] + [other]

    loads = []
    for o in range(n_tm):
        start = pl.multiple_of(flipped(tm, o) * own, own)
        load = pltpu.make_async_copy(p_hbm.at[pl.ds(start, own), :], p_all.at[o], load_sem.at[o])
        load.start()
        loads.append(load)
    own_load = pltpu.make_async_copy(s_hbm, s_all.at[0], s_load)
    own_load.start()

    barrier = pltpu.get_barrier_semaphore()
    for where in partners:
        pl.semaphore_signal(barrier, inc=1, device_id=where, device_id_type=MESH)
    pl.semaphore_wait(barrier, len(partners))

    def remote(src, dst, send, recv, where):
        copy = pltpu.make_async_remote_copy(
            src_ref=src, dst_ref=dst, send_sem=send, recv_sem=recv, device_id=where, device_id_type=MESH
        )
        copy.start()
        return copy

    low, high = pl.ds(0, own // 2), pl.ds(own // 2, own // 2)
    parts = (low, high)

    def send_sketch(o, h):
        return remote(s_hbm.at[parts[h], :], s_all.at[o, parts[h], :], s_send.at[o, h], s_recv.at[o, h], tm_partner(o))

    def forward_sketch(o, h):
        rows = s_all.at[o, parts[h], :]
        return remote(rows, s_all.at[3, parts[h], :], s_send.at[3, h], s_recv.at[3, h], tm_partner(3 - o))

    arrivals = {}
    if n_tm == 4:
        for o, h in ((1, 0), (2, 1), (1, 1), (2, 0)):
            arrivals[o, h] = send_sketch(o, h)
    else:
        for o in range(1, n_tm):
            for h in range(2):
                arrivals[o, h] = send_sketch(o, h)

    for o in range(n_tm):
        if o == 0:
            own_load.wait()
        else:
            if n_tm == 4 and o == 1:
                arrivals[1, 0].wait_recv()
                arrivals[3, 0] = forward_sketch(1, 0)
                arrivals[2, 1].wait_recv()
                arrivals[3, 1] = forward_sketch(2, 1)
                arrivals[1, 1].wait_recv()
            elif n_tm == 4 and o == 2:
                arrivals[2, 0].wait_recv()
            else:
                arrivals[o, 0].wait_recv()
                arrivals[o, 1].wait_recv()
        loads[o].wait()
        product = lax.dot_general(
            s_all[o], p_all[o], (((0,), (0,)), ((), ())), preferred_element_type=F32
        )
        if o == 0:
            yt[...] = product
        else:
            yt[...] += product

    mine = pl.multiple_of(core * half, half)
    theirs = pl.multiple_of((1 - core) * half, half)
    copy = remote(yt.at[pl.ds(theirs, half), :], core_in, c_send, c_recv, other)
    copy.wait()
    yt[pl.ds(mine, half), :] += core_in[...]
    at = pl.multiple_of(mine + z * piece, piece)
    copies = []
    for o in range(1, n_z):
        there = pl.multiple_of(mine + flipped(z, o) * piece, piece)
        copies.append(remote(yt.at[pl.ds(there, piece), :], z_in.at[o], z_send.at[o], z_recv.at[o], z_partner(o)))
    total = yt[pl.ds(at, piece), :]
    for o in range(1, n_z):
        copies[o - 1].wait()
        total = total + z_in[o]
    y_full[pl.ds(at, piece), :] = total
    gathered = y_full.at[pl.ds(at, piece), :]
    copies = [
        remote(gathered, gathered, a_send.at[o], a_recv.at[o], z_partner(o)) for o in range(1, n_z)
    ]
    for copy in copies:
        copy.wait()
    gathered = y_full.at[pl.ds(mine, half), :]
    remote(gathered, gathered, b_send, b_recv, other).wait()

    rows = y_full[...]
    g_own[...] = lax.dot_general(
        rows, rows, (((1,), (1,)), ((), ())), precision=HIGHEST, preferred_element_type=F32
    )
    copies = [
        remote(g_own, g_in.at[o], g_send.at[o], g_recv.at[o], tm_partner(o)) for o in range(1, n_tm)
    ]
    gram = g_own[...]
    for o in range(1, n_tm):
        copies[o - 1].wait()
        gram = gram + g_in[o]
    aug[:, :k] = gram
    aug[:, k:] = (
        lax.broadcasted_iota(jnp.int32, (k, k), 0) == lax.broadcasted_iota(jnp.int32, (k, k), 1)
    ).astype(F32)
    inverse_factor(aug, linv)
    basis_t = jnp.dot(linv[...], y_full[...], precision=HIGHEST, preferred_element_type=F32)
    basis[...] = basis_t.T.astype(BF16)
    basis_store = pltpu.make_async_copy(basis, basis_ref, store_sem.at[0])
    basis_store.start()

    def partial(o, h):
        return jnp.dot(p_all[o, parts[h], :], basis[...], preferred_element_type=F32)

    def send_image(block, o, h):
        out_part[o, parts[h], :] = block.astype(BF16)
        return remote(out_part.at[o, parts[h], :], in_part.at[o, parts[h], :],
                      o_send.at[o, h], o_recv.at[o, h], tm_partner(o))

    copies = {}
    if n_tm == 4:
        diagonal = 3
        for h in range(2):
            out_part[diagonal, parts[h], :] = partial(diagonal, h).astype(BF16)
            copies[diagonal, h] = remote(
                out_part.at[diagonal, parts[h], :], in_part.at[diagonal, parts[h], :],
                o_send.at[diagonal, h], o_recv.at[diagonal, h], tm_partner(1 + h),
            )
        for o, h in ((1, 0), (2, 1)):
            copies[o, h] = send_image(partial(o, h), o, h)
        for o, h in ((2, 0), (1, 1)):
            block = partial(o, h)
            copies[diagonal, h].wait_recv()
            copies[o, h] = send_image(block + in_part[diagonal, parts[h], :].astype(F32), o, h)
        taken = ((1, 0), (2, 1), (2, 0), (1, 1))
    else:
        taken = tuple((o, h) for o in range(n_tm - 1, 0, -1) for h in range(2))
        for o, h in taken:
            copies[o, h] = send_image(partial(o, h), o, h)
    for h in range(2):
        image[parts[h], :] = partial(0, h)
    for o, h in taken:
        copies[o, h].wait_recv()
        image[parts[h], :] += in_part[o, parts[h], :].astype(F32)
    store = pltpu.make_async_copy(image, image_ref, store_sem.at[1])
    store.start()
    for copy in list(arrivals.values()) + list(copies.values()):
        copy.wait_send()
    basis_store.wait()
    store.wait()


def on_device(n_panel, n_tm, pressures, sketch):
    own, k = sketch.shape
    nt = pressures.shape[1]
    n_z = n_panel // 2
    dma = pltpu.SemaphoreType.DMA
    return pl.pallas_call(
        functools.partial(kernel, n_panel, n_tm),
        out_shape=(jax.ShapeDtypeStruct((nt, k), BF16), jax.ShapeDtypeStruct((own, k), F32)),
        in_specs=[pl.BlockSpec(memory_space=pl.ANY)] * 2,
        out_specs=(pl.BlockSpec(memory_space=pl.ANY),) * 2,
        scratch_shapes=[
            pltpu.VMEM((n_tm, own, nt), BF16),
            pltpu.VMEM((n_tm, own, k), BF16),
            pltpu.VMEM((k, nt), F32),
            pltpu.VMEM((k, nt), F32),
            pltpu.VMEM((k // 2, nt), F32),
            pltpu.VMEM((n_z, k // n_panel, nt), F32),
            pltpu.VMEM((k, k), F32),
            pltpu.VMEM((n_tm, k, k), F32),
            pltpu.VMEM((k, 2 * k), F32),
            pltpu.VMEM((k, k), F32),
            pltpu.VMEM((nt, k), BF16),
            pltpu.VMEM((n_tm, own, k), BF16),
            pltpu.VMEM((n_tm, own, k), BF16),
            pltpu.VMEM((own, k), F32),
            dma((n_tm,)), dma, dma((n_tm, 2)), dma((n_tm, 2)),
            dma, dma, dma((n_z,)), dma((n_z,)), dma((n_z,)), dma((n_z,)),
            dma, dma, dma((n_tm,)), dma((n_tm,)), dma((n_tm, 2)), dma((n_tm, 2)), dma((2,)),
        ],
        compiler_params=pltpu.CompilerParams(
            collective_id=0, has_side_effects=True, vmem_limit_bytes=48 * 1024 * 1024
        ),
        cost_estimate=pl.CostEstimate(
            flops=4 * pressures.shape[0] * nt * k, bytes_accessed=2 * pressures.size, transcendentals=0
        ),
    )(pressures, sketch)


def solution(mesh):
    return jax.shard_map(
        functools.partial(on_device, mesh.shape["panel"], mesh.shape["tm"]),
        mesh=mesh,
        in_specs=(P("panel", "tm"), P(("panel", "tm"), None)),
        out_specs=(P("tm", None), P(("panel", "tm"), None)),
        check_vma=False,
    )
```
